256 devices in a mesh: grp: 8 (over y, core), dev: 32 (over z, x).
Axes of the slice: x: 4, y: 4, z: 8, core: 2. Of those that a mesh axis runs over, the one named last changes fastest.
Arguments:
- tokens: bfloat16 [6144, 512], P('dev', 'grp'), may hold values from -6 to 6
- d_out: bfloat16 [6144, 512], P('dev', 'grp'), may hold values from -6 to 6
- scores: float32 [512, 2], P('grp'), may hold values from -0.4 to 0.4
- expert_ids: int32 [512, 2], P('grp'), may hold values from 0 to 3, as said below
- w_gate: bfloat16 [6144, 32768], P(None, ('grp', 'dev')), may hold values from -0.078125 to 0.078125
- w_up: bfloat16 [6144, 32768], P(None, ('grp', 'dev')), may hold values from -0.078125 to 0.078125
- w_down: bfloat16 [6144, 32768], P(None, ('grp', 'dev')), may hold values from -0.0625 to 0.0625
Outputs:
- mixed: bfloat16 [6144, 512], P('dev', 'grp')
- d_tokens: bfloat16 [6144, 512], P('dev', 'grp')
- grad_gate: bfloat16 [6144, 32768], P(None, ('grp', 'dev'))
- grad_up: bfloat16 [6144, 32768], P(None, ('grp', 'dev'))
- grad_down: bfloat16 [6144, 32768], P(None, ('grp', 'dev'))
The draws below stay inside these ranges and needn't reach their ends.
Inputs may be any that keep to these rules, and one draw needn't show every extreme that they name: `expert_ids`: the two experts of a token differ; in every group of 64 tokens two of the experts are chosen by exactly 48 tokens each and the other experts by fewer.
All inputs are finite; a program needn't handle non-finite values.
Results may differ from the reference program's by a relative error of at most 0.035.
Values may be sent and summed in bfloat16 or wider, within the bound.
No kernel may reach another device: no remote copies, remote signals or barrier semaphores. Data moves between devices by JAX's collectives and lax.ppermute only.
A program may use at most 128 MiB of HBM per device.

```python
import jax
import jax.numpy as jnp
from jax import lax

D = 6144
FF = 8192
EXPERTS = 4
TOP = 2
TOK_GRP = 64
TOKENS = 512
HIDDEN_ALL = 32768
N_GRP = 8
N_DEV = 32


def draw_expert_ids(key, part):
    key = jax.random.fold_in(key, 11)
    group_total = TOKENS // TOK_GRP
    half_rows = TOK_GRP // 2
    quarter = TOK_GRP // 4

    def one_group(group_key):
        group_keys = jax.random.split(group_key, 4)
        expert_order = jax.random.permutation(group_keys[0], EXPERTS).astype(jnp.int32)
        first_heavy = expert_order[0]
        second_heavy = expert_order[1]
        light_pick = jax.random.randint(group_keys[1], (half_rows,), 2, EXPERTS)
        light_ids = expert_order[light_pick]
        heavy_ids = jnp.concatenate([jnp.full((quarter,), first_heavy, jnp.int32), jnp.full((quarter,), second_heavy, jnp.int32)])
        column_left = jnp.concatenate([jnp.full((half_rows,), first_heavy, jnp.int32), heavy_ids])
        column_right = jnp.concatenate([jnp.full((half_rows,), second_heavy, jnp.int32), light_ids])
        swap_bits = jax.random.randint(group_keys[2], (TOK_GRP,), 0, 2)
        left_final = jnp.where(swap_bits == 1, column_right, column_left)
        right_final = jnp.where(swap_bits == 1, column_left, column_right)
        chosen_pairs = jnp.stack([left_final, right_final], axis=1)
        shuffle_rows = jax.random.permutation(group_keys[3], TOK_GRP)
        return chosen_pairs[shuffle_rows].astype(jnp.int32)
    every_group = jax.vmap(one_group)(jax.random.split(key, group_total))
    return every_group.reshape(TOKENS, TOP).astype(jnp.int32)


def levels(own_key, dims, cuts, low, top_value):
    gain = 1.0
    for axis_at, parts in cuts:
        heights = jax.random.uniform(jax.random.fold_in(jax.random.fold_in(own_key, 6), axis_at), (parts,), jnp.float32, low / len(cuts), top_value / len(cuts))
        gain = gain * jnp.repeat(jnp.exp(heights), dims[axis_at] // parts).reshape((-1,) + (1,) * (len(dims) - 1 - axis_at))
    return gain


def gaussian(own_key, shape, deviation, reach, pieces=(), held_as=jnp.bfloat16):
    result = deviation * jax.random.normal(own_key, shape, jnp.float32)
    if pieces:
        result = result * levels(own_key, shape, pieces, -0.22, 0.18)
    return jnp.clip(result, -reach, reach).astype(held_as)


def setup_inputs(seed: int = 0) -> dict:
    key_list = jax.random.split(jax.random.key(seed), 8)
    tokens = gaussian(key_list[0], (D, TOKENS), 1.0, 6.0, ((0, 32), (1, 8)))
    d_out = gaussian(key_list[1], (D, TOKENS), 1.0, 6.0, ((0, 32), (1, 8)))
    scores = jnp.clip(jax.random.uniform(key_list[2], (TOKENS, TOP), jnp.float32, -0.4, 0.4) * levels(key_list[2], (TOKENS, TOP), ((0, 8),), -0.4, 0.0), -0.4, 0.4)
    expert_ids = draw_expert_ids(jax.random.fold_in(key_list[7], 71), 0)
    w_gate = gaussian(key_list[4], (D, HIDDEN_ALL), D ** -0.5, 0.078125, ((1, 256),))
    w_up = gaussian(key_list[5], (D, HIDDEN_ALL), D ** -0.5, 0.078125, ((1, 256),))
    w_down = gaussian(key_list[6], (D, HIDDEN_ALL), FF ** -0.5, 0.0625, ((1, 256),))
    return {"tokens": tokens, "d_out": d_out, "scores": scores, "expert_ids": expert_ids, "w_gate": w_gate, "w_up": w_up, "w_down": w_down}


def swish_parts(act_gate):
    sigmoid_gate = jax.nn.sigmoid(act_gate)
    return sigmoid_gate, act_gate * sigmoid_gate


def reference(tokens, d_out, scores, expert_ids, w_gate, w_up, w_down):
    spread = N_GRP // EXPERTS
    hidden_width = FF // (spread * N_DEV)
    gate_pair = jnp.stack([jax.nn.sigmoid(scores[:, 0] - scores[:, 1]), jax.nn.sigmoid(scores[:, 1] - scores[:, 0])], axis=1)
    token_rows = tokens.T
    cotangent = d_out.astype(jnp.float32)
    mixed_total = jnp.zeros((D, TOKENS), jnp.float32)
    back_total = jnp.zeros((D, TOKENS), jnp.float32)
    gate_collected, up_collected, down_collected = [], [], []
    for expert in range(EXPERTS):
        weighting = jnp.sum(jnp.where(expert_ids == expert, gate_pair, jnp.float32(0.0)), axis=1)
        scaled = (cotangent * weighting[None, :]).astype(jnp.bfloat16)
        scaled_rows = scaled.T
        expert_total = jnp.zeros((D, TOKENS), jnp.float32)
        for half_index in range(spread):
            base_slice = (expert * spread + half_index) * N_DEV

            def one_slice(totals, device_index):
                offset = ((base_slice + device_index) * hidden_width).astype(jnp.int32)
                gate_cols = lax.dynamic_slice_in_dim(w_gate, offset, hidden_width, 1)
                up_cols = lax.dynamic_slice_in_dim(w_up, offset, hidden_width, 1)
                down_cols = lax.dynamic_slice_in_dim(w_down, offset, hidden_width, 1)
                act_gate = jnp.dot(token_rows, gate_cols, preferred_element_type=jnp.float32)
                act_up = jnp.dot(token_rows, up_cols, preferred_element_type=jnp.float32)
                sigmoid_gate, swished = swish_parts(act_gate)
                hidden = (swished * act_up).astype(jnp.bfloat16)
                out_part = jnp.dot(down_cols, hidden.T, preferred_element_type=jnp.float32).astype(jnp.bfloat16)
                back_hidden = jnp.dot(scaled_rows, down_cols, preferred_element_type=jnp.float32)
                grad_act = (back_hidden * act_up * sigmoid_gate * (1.0 + act_gate * (1.0 - sigmoid_gate))).astype(jnp.bfloat16)
                grad_lin = (back_hidden * swished).astype(jnp.bfloat16)
                grad_down = jnp.dot(scaled, hidden, preferred_element_type=jnp.float32).astype(jnp.bfloat16)
                grad_gate = jnp.dot(tokens, grad_act, preferred_element_type=jnp.float32).astype(jnp.bfloat16)
                grad_up = jnp.dot(tokens, grad_lin, preferred_element_type=jnp.float32).astype(jnp.bfloat16)
                back_part = (jnp.dot(gate_cols, grad_act.T, preferred_element_type=jnp.float32) + jnp.dot(up_cols, grad_lin.T, preferred_element_type=jnp.float32)).astype(jnp.bfloat16)
                out_part, back_part = lax.optimization_barrier((out_part, back_part))
                return (totals[0] + out_part.astype(jnp.float32), totals[1] + back_part.astype(jnp.float32)), (grad_gate, grad_up, grad_down)

            zero_field = jnp.zeros((D, TOKENS), jnp.float32)
            (out_run, back_run), slice_grads = lax.scan(one_slice, (zero_field, zero_field), jnp.arange(N_DEV, dtype=jnp.int32))
            out_run, back_run = lax.optimization_barrier((out_run.astype(jnp.bfloat16), back_run.astype(jnp.bfloat16)))
            expert_total = expert_total + out_run.astype(jnp.float32)
            back_total = back_total + back_run.astype(jnp.float32)
            for collected, stacked in zip((gate_collected, up_collected, down_collected), slice_grads):
                collected.append(jnp.transpose(stacked, (1, 0, 2)).reshape(D, N_DEV * hidden_width))
        mixed_total = mixed_total + weighting[None, :] * expert_total
    return (mixed_total.astype(jnp.bfloat16), back_total.astype(jnp.bfloat16), jnp.concatenate(gate_collected, axis=1), jnp.concatenate(up_collected, axis=1), jnp.concatenate(down_collected, axis=1))
```

```python
import jax
import jax.numpy as jnp
from jax import lax
from jax.sharding import Mesh, PartitionSpec as P

EXPERTS = 4
TOK_GRP = 64
CAP = 48
F32 = jnp.float32
BF16 = jnp.bfloat16


def shift(n, k):
    return [(i, (i + k) % n) for i in range(n)]


def dot(a, b, dims):
    return lax.dot_general(a, b, (dims, ((), ())), preferred_element_type=F32)


def swap(a):
    return lax.ppermute(a, "core", [(0, 1), (1, 0)])


def body(tokens, d_out, scores, expert_ids, w_gate, w_up, w_down):
    nz, nx = lax.axis_size("z"), lax.axis_size("x")
    z, x, core = lax.axis_index("z"), lax.axis_index("x"), lax.axis_index("core")
    rows = tokens.shape[0]
    half = rows // 2
    hid = w_gate.shape[1]
    slots = CAP * 8

    def split(w):
        parts = w.reshape(nz * nx, 2, half, hid)
        own = lax.dynamic_index_in_dim(parts, core, 1, keepdims=False)
        other = lax.dynamic_index_in_dim(parts, 1 - core, 1, keepdims=False)
        return own.reshape(-1, hid), other.reshape(-1, hid)

    w_own, w_other = zip(*(split(w) for w in (w_gate, w_up, w_down)))
    w_far = swap(jnp.stack(w_other))
    both = [
        jnp.concatenate(
            [jnp.where(core == 0, o, f), jnp.where(core == 0, f, o)], axis=1
        ).reshape(nz, nx * half, 2 * hid)
        for o, f in zip(w_own, (w_far[0], w_far[1], w_far[2]))
    ]
    wg, wu, wd = both

    gate_first = jax.nn.sigmoid(scores[:, 0] - scores[:, 1])
    gate_second = jax.nn.sigmoid(scores[:, 1] - scores[:, 0])
    labels = jnp.arange(EXPERTS, dtype=jnp.int32)
    chosen_first = (expert_ids[:, 0:1] == labels[None, :]).astype(jnp.int32)
    chosen_second = (expert_ids[:, 1:2] == labels[None, :]).astype(jnp.int32)
    counts = chosen_first + chosen_second
    earlier = jnp.arange(TOK_GRP)[:, None] > jnp.arange(TOK_GRP)[None, :]
    rank_table = dot(earlier.astype(BF16), counts.astype(BF16), ((1,), (0,))).astype(jnp.int32)
    slot_first = jnp.sum(rank_table * chosen_first, axis=1)
    slot_second = jnp.sum(rank_table * chosen_second, axis=1)
    place_first = expert_ids[:, 0] * CAP + slot_first
    place_second = expert_ids[:, 1] * CAP + slot_second
    places = jnp.arange(EXPERTS * CAP, dtype=jnp.int32)
    sel_first = place_first[:, None] == places[None, :]
    sel_second = place_second[:, None] == places[None, :]
    sel_both = (sel_first | sel_second).astype(BF16)
    slot_gate = jnp.sum(
        jnp.where(sel_first, gate_first[:, None], 0.0)
        + jnp.where(sel_second, gate_second[:, None], 0.0),
        axis=0,
    )
    sent_t = dot(sel_both, tokens, ((0,), (1,))).astype(BF16)
    sent_d = (dot(sel_both, d_out, ((0,), (1,))) * slot_gate[:, None]).astype(BF16)
    sent = jnp.stack(
        [sent_t.reshape(EXPERTS, CAP, 2, half), sent_d.reshape(EXPERTS, CAP, 2, half)], axis=3
    )
    sent = sent.transpose(0, 2, 1, 3, 4).reshape(EXPERTS * 2, CAP, 2 * half)
    got = lax.all_to_all(sent, ("y", "core"), 0, 0, tiled=True)
    shard = got.reshape(slots, 2, half).transpose(1, 2, 0)

    row = jnp.zeros((2, nx, half, slots), BF16)

    def put_x(row, piece, k):
        return lax.dynamic_update_slice(row, piece[:, None], (0, lax.rem(x - k + nx, nx), 0, 0))

    pieces = [shard] + [lax.ppermute(shard, "x", shift(nx, k)) for k in range(1, nx)]
    for k, piece in enumerate(pieces):
        row = put_x(row, piece, k)
    row = row.reshape(2, nx * half, slots)

    acts = [jnp.zeros((2 * hid, slots), F32) for _ in range(3)]
    full_t = jnp.zeros((nz, nx * half, slots), BF16)
    full_d = jnp.zeros((nz, nx * half, slots), BF16)

    def use(state, block, src):
        ft, fd, a = state
        t, d = block[0], block[1]
        a = [
            a[0] + dot(lax.dynamic_index_in_dim(wg, src, 0, keepdims=False), t, ((0,), (0,))),
            a[1] + dot(lax.dynamic_index_in_dim(wu, src, 0, keepdims=False), t, ((0,), (0,))),
            a[2] + dot(lax.dynamic_index_in_dim(wd, src, 0, keepdims=False), d, ((0,), (0,))),
        ]
        ft = lax.dynamic_update_slice(ft, t[None], (src, 0, 0))
        fd = lax.dynamic_update_slice(fd, d[None], (src, 0, 0))
        return ft, fd, a

    state = (full_t, full_d, acts)
    right = left = row
    for k in range(nz // 2):
        if k < nz // 2 - 1:
            next_right = lax.ppermute(right, "z", shift(nz, 1))
            next_left = lax.ppermute(left, "z", shift(nz, -1))
        else:
            next_right = lax.ppermute(right[0], "z", shift(nz, 1))
            next_left = lax.ppermute(left[1], "z", shift(nz, -1))
        state = use(state, right, lax.rem(z - k + nz, nz))
        if k > 0:
            state = use(state, left, lax.rem(z + k, nz))
        right, left = next_right, next_left
    last = jnp.stack([right, left])
    full_t, full_d, acts = use(state, last, lax.rem(z + nz // 2, nz))
    full_t = full_t.reshape(-1, slots)
    full_d = full_d.reshape(-1, slots)

    acts = jnp.stack(acts).reshape(3, 2, hid, slots)
    mine = lax.dynamic_index_in_dim(acts, core, 1, keepdims=False)
    theirs = lax.dynamic_index_in_dim(acts, 1 - core, 1, keepdims=False)
    mine = mine + swap(theirs)
    act_gate, act_up, back_hidden = mine[0], mine[1], mine[2]
    sig = jax.nn.sigmoid(act_gate)
    swished = act_gate * sig
    hidden = (swished * act_up).astype(BF16)
    grad_act = (back_hidden * act_up * sig * (1.0 + act_gate * (1.0 - sig))).astype(BF16)
    grad_lin = (back_hidden * swished).astype(BF16)
    own = jnp.stack([hidden, grad_act, grad_lin])
    far = swap(own)
    pair = jnp.concatenate(
        [jnp.where(core == 0, own, far), jnp.where(core == 0, far, own)], axis=1
    )
    hidden, grad_act, grad_lin = pair[0], pair[1], pair[2]

    def made(dest):
        at = lambda w: lax.dynamic_index_in_dim(w, dest, 0, keepdims=False)
        out = dot(at(wd), hidden, ((1,), (0,)))
        back = dot(at(wg), grad_act, ((1,), (0,))) + dot(at(wu), grad_lin, ((1,), (0,)))
        return jnp.stack([out, back])

    far_block = made(lax.rem(z + nz // 2, nz)).astype(BF16)
    right = lax.ppermute(far_block[0], "z", shift(nz, 1))
    left = lax.ppermute(far_block[1], "z", shift(nz, -1))
    for k in range(nz // 2 - 1, 0, -1):
        to_right = made(lax.rem(z + k, nz))
        to_left = made(lax.rem(z - k + nz, nz))
        if k == nz // 2 - 1:
            to_right = jnp.stack([to_right[0] + right.astype(F32), to_right[1]])
            to_left = jnp.stack([to_left[0], to_left[1] + left.astype(F32)])
        else:
            to_right = to_right + right.astype(F32)
            to_left = to_left + left.astype(F32)
        right = lax.ppermute(to_right.astype(BF16), "z", shift(nz, 1))
        left = lax.ppermute(to_left.astype(BF16), "z", shift(nz, -1))
    total = (made(z) + right.astype(F32) + left.astype(F32)).reshape(2, nx, half, slots)
    total_b = total.astype(BF16)
    pick = lambda a, i: lax.dynamic_index_in_dim(a, i, 1, keepdims=False)
    result = pick(total, x)
    for k in range(1, nx):
        sent_piece = pick(total_b, lax.rem(x + k, nx))
        result = result + lax.ppermute(sent_piece, "x", shift(nx, k)).astype(F32)
    result = result.astype(BF16)

    back_sent = result.transpose(2, 0, 1).reshape(8, CAP, 2 * half)
    back_got = lax.all_to_all(back_sent, ("y", "core"), 0, 0, tiled=True)
    back_got = back_got.reshape(EXPERTS, 2, CAP, 2, half).transpose(3, 1, 4, 0, 2)
    back_got = back_got.reshape(2, rows, EXPERTS * CAP)
    out_first = dot(back_got[0], sel_first.astype(BF16), ((1,), (1,)))
    out_second = dot(back_got[0], sel_second.astype(BF16), ((1,), (1,)))
    mixed = (out_first * gate_first[None, :] + out_second * gate_second[None, :]).astype(BF16)
    d_tokens = dot(back_got[1], sel_both, ((1,), (1,))).astype(BF16)

    grads = [
        dot(full, g, ((1,), (1,))).astype(BF16)
        for full, g in ((full_t, grad_act), (full_t, grad_lin), (full_d, hidden))
    ]
    keep = [lax.dynamic_slice_in_dim(g, core * hid, hid, 1) for g in grads]
    give = [lax.dynamic_slice_in_dim(g, (1 - core) * hid, hid, 1) for g in grads]
    come = [swap(g) for g in give]
    done = []
    for k, c in zip(keep, come):
        k, c = k.reshape(nz * nx, half, hid), c.reshape(nz * nx, half, hid)
        done.append(
            jnp.stack([jnp.where(core == 0, k, c), jnp.where(core == 0, c, k)], axis=1).reshape(
                nz * nx * rows, hid
            )
        )
    return (mixed, d_tokens, done[0], done[1], done[2])


def solution(mesh):
    fine = Mesh(mesh.devices.reshape(4, 2, 8, 4), ("y", "core", "z", "x"))
    shard = P(("z", "x"), ("y", "core"))
    group = P(("y", "core"), None)
    weight = P(None, ("y", "core", "z", "x"))
    return jax.shard_map(
        body,
        mesh=fine,
        in_specs=(shard, shard, group, group, weight, weight, weight),
        out_specs=(shard, shard, weight, weight, weight),
        check_vma=False,
    )
```

```python
import jax
import jax.numpy as jnp
from jax import lax
from jax.sharding import Mesh, PartitionSpec as P

EXPERTS = 4
TOK_GRP = 64
CAP = 48
F32 = jnp.float32
BF16 = jnp.bfloat16


def shift(n, k):
    return [(i, (i + k) % n) for i in range(n)]


def dot(a, b, dims):
    return lax.dot_general(a, b, (dims, ((), ())), preferred_element_type=F32)


def swap(a):
    return lax.ppermute(a, "core", [(0, 1), (1, 0)])


def body(tokens, d_out, scores, expert_ids, w_gate, w_up, w_down):
    nz, nx = lax.axis_size("z"), lax.axis_size("x")
    z, x, core = lax.axis_index("z"), lax.axis_index("x"), lax.axis_index("core")
    rows = tokens.shape[0]
    half = rows // 2
    hid = w_gate.shape[1]
    slots = CAP * 8

    def split(w):
        parts = w.reshape(nz, nx, 2, half, hid)
        own = lax.dynamic_index_in_dim(parts, core, 2, keepdims=False)
        other = lax.dynamic_index_in_dim(parts, 1 - core, 2, keepdims=False)
        return jnp.roll(own, -x, axis=1), jnp.roll(other, -x, axis=1)

    def whole(own, far):
        pair = [jnp.where(core == 0, own, far), jnp.where(core == 0, far, own)]
        return jnp.concatenate(pair, axis=-1)

    wg, wu, wd = [
        whole(own, swap(other)) for own, other in (split(w) for w in (w_gate, w_up, w_down))
    ]

    gate_first = jax.nn.sigmoid(scores[:, 0] - scores[:, 1])
    gate_second = jax.nn.sigmoid(scores[:, 1] - scores[:, 0])
    labels = jnp.arange(EXPERTS, dtype=jnp.int32)
    chosen_first = (expert_ids[:, 0:1] == labels[None, :]).astype(jnp.int32)
    chosen_second = (expert_ids[:, 1:2] == labels[None, :]).astype(jnp.int32)
    counts = chosen_first + chosen_second
    earlier = jnp.arange(TOK_GRP)[:, None] > jnp.arange(TOK_GRP)[None, :]
    rank_table = dot(earlier.astype(BF16), counts.astype(BF16), ((1,), (0,))).astype(jnp.int32)
    slot_first = jnp.sum(rank_table * chosen_first, axis=1)
    slot_second = jnp.sum(rank_table * chosen_second, axis=1)
    place_first = expert_ids[:, 0] * CAP + slot_first
    place_second = expert_ids[:, 1] * CAP + slot_second
    places = jnp.arange(EXPERTS * CAP, dtype=jnp.int32)
    sel_first = place_first[:, None] == places[None, :]
    sel_second = place_second[:, None] == places[None, :]
    sel_both = (sel_first | sel_second).astype(BF16)
    slot_gate = jnp.sum(
        jnp.where(sel_first, gate_first[:, None], 0.0)
        + jnp.where(sel_second, gate_second[:, None], 0.0),
        axis=0,
    )
    sent_t = dot(sel_both, tokens, ((0,), (1,))).astype(BF16)
    sent_d = (dot(sel_both, d_out, ((0,), (1,))) * slot_gate[:, None]).astype(BF16)
    sent = jnp.stack(
        [sent_t.reshape(EXPERTS, CAP, 2, half), sent_d.reshape(EXPERTS, CAP, 2, half)], axis=3
    )
    sent = sent.transpose(0, 2, 1, 3, 4).reshape(EXPERTS * 2, CAP, 2 * half)
    got = lax.all_to_all(sent, ("y", "core"), 0, 0, tiled=True)
    eye = (
        lax.broadcasted_iota(jnp.int32, (slots, slots), 0)
        == lax.broadcasted_iota(jnp.int32, (slots, slots), 1)
    ).astype(BF16)
    shard = dot(got.reshape(slots, 2 * half), eye, ((0,), (0,))).astype(BF16)
    shard_t, shard_d = shard[:half], shard[half:]

    def along_x(piece):
        pieces = [piece] + [lax.ppermute(piece, "x", shift(nx, -k)) for k in range(1, nx)]
        return jnp.concatenate(pieces, axis=0)

    block = nx * half

    def weights(w, at):
        return lax.dynamic_index_in_dim(w, at, 0, keepdims=False).reshape(block, 2 * hid)

    def ring(row, use, late=None):
        right = left = row
        mark = None
        for k in range(nz // 2):
            if k < nz // 2 - 1:
                next_right = lax.ppermute(right, "z", shift(nz, 1))
                next_left = lax.ppermute(left, "z", shift(nz, -1))
            else:
                mark = (right, left)
                next_right = lax.ppermute(right[: block // 2], "z", shift(nz, 1))
                next_left = lax.ppermute(left[block // 2 :], "z", shift(nz, -1))
            use(right, lax.rem(z - k + nz, nz))
            if k > 0:
                use(left, lax.rem(z + k, nz))
            right, left = next_right, next_left
        use(jnp.concatenate([right, left]), lax.rem(z + nz // 2, nz))
        return mark

    full_t = [jnp.zeros((nz, block, slots), BF16)]
    full_d = [jnp.zeros((nz, block, slots), BF16)]
    acts = [jnp.zeros((2 * hid, slots), F32) for _ in range(3)]

    def use_t(t, src):
        full_t[0] = lax.dynamic_update_slice(full_t[0], t[None], (src, 0, 0))
        acts[0] = acts[0] + dot(weights(wg, src), t, ((0,), (0,)))
        acts[1] = acts[1] + dot(weights(wu, src), t, ((0,), (0,)))

    def use_d(d, src):
        full_d[0] = lax.dynamic_update_slice(full_d[0], d[None], (src, 0, 0))
        acts[2] = acts[2] + dot(weights(wd, src), d, ((0,), (0,)))

    def finish(parts):
        parts = jnp.stack(parts).reshape(len(parts), 2, hid, slots)
        mine = lax.dynamic_index_in_dim(parts, core, 1, keepdims=False)
        theirs = lax.dynamic_index_in_dim(parts, 1 - core, 1, keepdims=False)
        return mine + swap(theirs)

    def share(own):
        far = swap(own)
        return jnp.concatenate(
            [jnp.where(core == 0, own, far), jnp.where(core == 0, far, own)], axis=-2
        )

    row_t = along_x(shard_t)
    shard_d, row_t = lax.optimization_barrier((shard_d, row_t))
    row_d = along_x(shard_d)
    mark = ring(row_t, use_t)
    row_d, _ = lax.optimization_barrier((row_d, mark))

    act_gate, act_up = finish(acts[:2])
    sig = jax.nn.sigmoid(act_gate)
    swished = act_gate * sig
    hidden = share((swished * act_up).astype(BF16))

    out = 0.0
    for k in list(range(1, nx)) + [0]:
        piece = dot(wd[:, k].reshape(nz * half, 2 * hid), hidden, ((1,), (0,)))
        if k:
            piece = lax.ppermute(piece.astype(BF16), "x", shift(nx, k)).astype(F32)
        out = out + piece
    out = out.astype(BF16).reshape(nz, half, slots)

    ring(row_d, use_d)
    back_hidden = finish(acts[2:])[0]
    grad_act = (back_hidden * act_up * sig * (1.0 + act_gate * (1.0 - sig))).astype(BF16)
    grad_lin = (back_hidden * swished).astype(BF16)
    pair = share(jnp.stack([grad_act, grad_lin]))
    grad_act, grad_lin = pair[0], pair[1]

    def made(dest):
        back = dot(weights(wg, dest), grad_act, ((1,), (0,))) + dot(
            weights(wu, dest), grad_lin, ((1,), (0,))
        )
        out_block = lax.dynamic_index_in_dim(out, dest, 0, keepdims=False).astype(F32)
        return jnp.concatenate([back, out_block], axis=0)

    cut = (nx + 1) * half // 2
    far_block = made(lax.rem(z + nz // 2, nz)).astype(BF16)
    right = lax.ppermute(far_block[:cut], "z", shift(nz, 1))
    left = lax.ppermute(far_block[cut:], "z", shift(nz, -1))
    for k in range(nz // 2 - 1, 0, -1):
        to_right = made(lax.rem(z + k, nz))
        to_left = made(lax.rem(z - k + nz, nz))
        if k == nz // 2 - 1:
            right, left, grad_act, grad_lin, hidden = lax.optimization_barrier(
                (right, left, grad_act, grad_lin, hidden)
            )
            to_right = jnp.concatenate([to_right[:cut] + right.astype(F32), to_right[cut:]])
            to_left = jnp.concatenate([to_left[:cut], to_left[cut:] + left.astype(F32)])
        else:
            to_right = to_right + right.astype(F32)
            to_left = to_left + left.astype(F32)
        right = lax.ppermute(to_right.astype(BF16), "z", shift(nz, 1))
        left = lax.ppermute(to_left.astype(BF16), "z", shift(nz, -1))
    total = made(z) + right.astype(F32) + left.astype(F32)
    total_b = total[:block].astype(BF16)
    back = total[:half]
    for k in range(1, nx):
        piece = total_b[k * half : (k + 1) * half]
        back = back + lax.ppermute(piece, "x", shift(nx, k)).astype(F32)
    result = jnp.concatenate([total[block:], back], axis=0).astype(BF16)

    back_sent = dot(result, eye[: 2 * half, : 2 * half], ((0,), (0,))).astype(BF16)
    back_sent = back_sent.reshape(8, CAP, 2 * half)
    back_got = lax.all_to_all(back_sent, ("y", "core"), 0, 0, tiled=True)
    back_got = back_got.reshape(EXPERTS, 2, CAP, 2, half).transpose(3, 1, 4, 0, 2)
    back_got = back_got.reshape(2, rows, EXPERTS * CAP)
    out_first = dot(back_got[0], sel_first.astype(BF16), ((1,), (1,)))
    out_second = dot(back_got[0], sel_second.astype(BF16), ((1,), (1,)))
    mixed = (out_first * gate_first[None, :] + out_second * gate_second[None, :]).astype(BF16)
    d_tokens = dot(back_got[1], sel_both, ((1,), (1,))).astype(BF16)

    done = []
    for full, g in ((full_t[0], grad_act), (full_t[0], grad_lin), (full_d[0], hidden)):
        grad = dot(full.reshape(-1, slots), g, ((1,), (1,))).astype(BF16)
        grad = jnp.roll(grad.reshape(nz, nx, half, 2 * hid), x, axis=1)
        keep = lax.dynamic_slice_in_dim(grad, core * hid, hid, 3)
        come = swap(lax.dynamic_slice_in_dim(grad, (1 - core) * hid, hid, 3))
        pair = [jnp.where(core == 0, keep, come), jnp.where(core == 0, come, keep)]
        done.append(jnp.stack(pair, axis=2).reshape(nz * nx * rows, hid))
    return (mixed, d_tokens, done[0], done[1], done[2])


def solution(mesh):
    fine = Mesh(mesh.devices.reshape(4, 2, 8, 4), ("y", "core", "z", "x"))
    shard = P(("z", "x"), ("y", "core"))
    group = P(("y", "core"), None)
    weight = P(None, ("y", "core", "z", "x"))
    return jax.shard_map(
        body,
        mesh=fine,
        in_specs=(shard, shard, group, group, weight, weight, weight),
        out_specs=(shard, shard, weight, weight, weight),
        check_vma=False,
    )
```

```python
import jax
import jax.numpy as jnp
from jax import lax
from jax.sharding import Mesh, PartitionSpec as P

EXPERTS = 4
TOK_GRP = 64
CAP = 48
F32 = jnp.float32
BF16 = jnp.bfloat16


def shift(n, k):
    return [(i, (i + k) % n) for i in range(n)]


def dot(a, b, dims):
    return lax.dot_general(a, b, (dims, ((), ())), preferred_element_type=F32)


def swap(a):
    return lax.ppermute(a, "core", [(0, 1), (1, 0)])


def body(tokens, d_out, scores, expert_ids, w_gate, w_up, w_down):
    nz, nx = lax.axis_size("z"), lax.axis_size("x")
    z, x, core = lax.axis_index("z"), lax.axis_index("x"), lax.axis_index("core")
    rows = tokens.shape[0]
    half = rows // 2
    hid = w_gate.shape[1]
    slots = CAP * 8
    block = nx * half
    mid = nz // 2

    def after(a, b):
        return lax.optimization_barrier((a, b))[0]

    gate_first = jax.nn.sigmoid(scores[:, 0] - scores[:, 1])
    gate_second = jax.nn.sigmoid(scores[:, 1] - scores[:, 0])
    labels = jnp.arange(EXPERTS, dtype=jnp.int32)
    chosen_first = (expert_ids[:, 0:1] == labels[None, :]).astype(jnp.int32)
    chosen_second = (expert_ids[:, 1:2] == labels[None, :]).astype(jnp.int32)
    counts = chosen_first + chosen_second
    earlier = jnp.arange(TOK_GRP)[:, None] > jnp.arange(TOK_GRP)[None, :]
    rank_table = dot(earlier.astype(BF16), counts.astype(BF16), ((1,), (0,))).astype(jnp.int32)
    slot_first = jnp.sum(rank_table * chosen_first, axis=1)
    slot_second = jnp.sum(rank_table * chosen_second, axis=1)
    place_first = expert_ids[:, 0] * CAP + slot_first
    place_second = expert_ids[:, 1] * CAP + slot_second
    places = jnp.arange(EXPERTS * CAP, dtype=jnp.int32)
    sel_first = place_first[:, None] == places[None, :]
    sel_second = place_second[:, None] == places[None, :]
    sel_both = (sel_first | sel_second).astype(BF16)
    slot_gate = jnp.sum(
        jnp.where(sel_first, gate_first[:, None], 0.0)
        + jnp.where(sel_second, gate_second[:, None], 0.0),
        axis=0,
    )
    scale = jnp.where(
        lax.broadcasted_iota(jnp.int32, (EXPERTS * CAP, 2 * half), 1) < half,
        1.0,
        slot_gate[:, None],
    )
    sent = []
    for part in range(2):
        own = slice(part * half, (part + 1) * half)
        both = jnp.concatenate([tokens[own], d_out[own]])
        sent.append((dot(sel_both, both, ((0,), (1,))) * scale).astype(BF16))
    sent = jnp.stack([a.reshape(EXPERTS, CAP, 2 * half) for a in sent], axis=1)
    sent = sent.reshape(EXPERTS * 2, CAP, 2 * half)
    got = lax.all_to_all(sent, ("y", "core"), 0, 0, tiled=True)
    w_gate, w_up, w_down = after((w_gate, w_up, w_down), got)
    eye = (
        lax.broadcasted_iota(jnp.int32, (slots, slots), 0)
        == lax.broadcasted_iota(jnp.int32, (slots, slots), 1)
    ).astype(BF16)
    shard = dot(got.reshape(slots, 2 * half), eye, ((0,), (0,))).astype(BF16)
    shard_t, shard_d = shard[:half], shard[half:]

    def prepare(w):
        parts = w.reshape(nz, nx, 2, half, hid)
        twice = jnp.concatenate([parts, parts], axis=1)

        def of(c):
            return lax.dynamic_slice(twice, (0, x, c, 0, 0), (nz, nx, 1, half, hid))[:, :, 0]

        return jnp.concatenate([of(core), swap(of(1 - core))], axis=-1)

    wg, wu, wd = prepare(w_gate), prepare(w_up), prepare(w_down)

    def at_z(a, j):
        return lax.dynamic_index_in_dim(a, lax.rem(z + j, nz), 0, keepdims=False)

    def of_z(w, j):
        return at_z(w, j).reshape(block, 2 * hid)

    def of_x(w, k):
        return w[:, k].reshape(nz * half, 2 * hid)

    def right_of(a):
        return lax.ppermute(a, "z", shift(nz, 1))

    def left_of(a):
        return lax.ppermute(a, "z", shift(nz, -1))

    def finish(parts):
        mine = jnp.stack([p[:hid] for p in parts])
        return mine + swap(jnp.stack([p[hid:] for p in parts]))

    def share(own):
        return jnp.concatenate([own, swap(own)], axis=-2)

    pieces = [shard_t] + [lax.ppermute(shard_t, "x", shift(nx, -k)) for k in range(1, nx)]
    blocks = [None] * nz
    right = left = blocks[0] = jnp.concatenate(pieces + [shard_d])
    cut = (block + half) // 2
    for k in range(1, mid):
        right, left = right_of(right), left_of(left)
        blocks[nz - k], blocks[k] = right, left
    blocks[mid] = jnp.concatenate([right_of(right[:cut]), left_of(left[cut:])])

    own_d = jnp.roll(jnp.stack([b[block:] for b in blocks]), z, axis=0).reshape(-1, slots)
    far_d = [lax.ppermute(own_d, "x", shift(nx, -k)) for k in range(1, nx)]

    acts = [0.0, 0.0]
    full_t = jnp.zeros((nz, block, slots), BF16)
    order = [0] + [j for k in range(1, mid) for j in (nz - k, k)] + [mid]
    for j in order:
        t = blocks[j][:block]
        acts[0] = acts[0] + dot(of_z(wg, j), t, ((0,), (0,)))
        acts[1] = acts[1] + dot(of_z(wu, j), t, ((0,), (0,)))
        full_t = lax.dynamic_update_slice(full_t, t[None], (lax.rem(z + j, nz), 0, 0))
    full_t = full_t.reshape(-1, slots)
    act_gate, act_up = finish(acts)
    sig = jax.nn.sigmoid(act_gate)
    swished = act_gate * sig
    hidden = share((swished * act_up).astype(BF16))

    def reduce_z(made, hold):
        far_block = made(mid).astype(BF16)
        middle = far_block.shape[0] // 2
        right, left = right_of(far_block[:middle]), left_of(far_block[middle:])
        for k in range(mid - 1, 0, -1):
            to_right, to_left = made(k), made(nz - k)
            if k == mid - 1:
                to_right = jnp.concatenate(
                    [to_right[:middle] + right.astype(F32), to_right[middle:]]
                )
                to_left = jnp.concatenate(
                    [to_left[:middle], to_left[middle:] + left.astype(F32)]
                )
            else:
                to_right = to_right + right.astype(F32)
                to_left = to_left + left.astype(F32)
            to_right, to_left = to_right.astype(BF16), to_left.astype(BF16)
            hold(k, to_right, to_left)
            right, left = right_of(to_right), left_of(to_left)
        return made(0) + right.astype(F32) + left.astype(F32)

    held = [far_d]

    def hold_d(k, right, left):
        if k == 2:
            held[0] = after(held[0], (right, left))

    out_row = reduce_z(lambda j: dot(of_z(wd, j), hidden, ((1,), (0,))), hold_d)
    all_d = [own_d] + list(held[0])
    back_hidden = 0.0
    for k in (0, 1, 3, 2):
        back_hidden = back_hidden + dot(of_x(wd, k), all_d[k], ((0,), (0,)))
    back_hidden = finish([back_hidden])[0]
    grad_act = (back_hidden * act_up * sig * (1.0 + act_gate * (1.0 - sig))).astype(BF16)
    grad_lin = (back_hidden * swished).astype(BF16)
    pair = share(jnp.stack([grad_act, grad_lin]))
    grad_act, grad_lin = pair[0], pair[1]

    def made_back(j):
        return dot(of_z(wg, j), grad_act, ((1,), (0,))) + dot(
            of_z(wu, j), grad_lin, ((1,), (0,))
        )

    for_grads = {}

    def hold_grads(k, right, left):
        for_grads[k] = after((grad_act, grad_lin, hidden)[mid - 1 - k], (right, left))

    back_row = reduce_z(made_back, hold_grads)

    rows_of = [
        jnp.concatenate([r[k * half : (k + 1) * half] for r in (out_row, back_row)])
        for k in range(nx)
    ]
    result = rows_of[0]
    for k in range(1, nx):
        piece = rows_of[k].astype(BF16)
        result = result + lax.ppermute(piece, "x", shift(nx, k)).astype(F32)
    result = result.astype(BF16)

    back_sent = dot(result, eye[: 2 * half, : 2 * half], ((0,), (0,))).astype(BF16)
    back_sent = back_sent.reshape(8, CAP, 2 * half)
    back_got = lax.all_to_all(back_sent, ("y", "core"), 0, 0, tiled=True)
    back_got = back_got.reshape(EXPERTS, 2, CAP, 2, half).transpose(3, 1, 4, 0, 2)
    back_got = back_got.reshape(2, rows, EXPERTS * CAP)
    out_first = dot(back_got[0], sel_first.astype(BF16), ((1,), (1,)))
    out_second = dot(back_got[0], sel_second.astype(BF16), ((1,), (1,)))
    mixed = (out_first * gate_first[None, :] + out_second * gate_second[None, :]).astype(BF16)
    d_tokens = dot(back_got[1], sel_both, ((1,), (1,))).astype(BF16)

    full_d = jnp.stack([a.reshape(nz, half, slots) for a in all_d], axis=1).reshape(-1, slots)
    which = lax.broadcasted_iota(jnp.int32, (nz, nx, 2, half, hid), 2)
    done = []
    for full, k in ((full_t, 3), (full_t, 2), (full_d, 1)):
        grad = dot(full, for_grads[k], ((1,), (1,))).astype(BF16)
        keep, give = grad[:, :hid], grad[:, hid:]
        keep, come = [
            jnp.roll(g.reshape(nz, nx, 1, half, hid), x, axis=1) for g in (keep, swap(give))
        ]
        done.append(jnp.where(which == core, keep, come).reshape(nz * nx * rows, hid))
    return (mixed, d_tokens, done[0], done[1], done[2])


def solution(mesh):
    fine = Mesh(mesh.devices.reshape(4, 2, 8, 4), ("y", "core", "z", "x"))
    shard = P(("z", "x"), ("y", "core"))
    group = P(("y", "core"), None)
    weight = P(None, ("y", "core", "z", "x"))
    return jax.shard_map(
        body,
        mesh=fine,
        in_specs=(shard, shard, group, group, weight, weight, weight),
        out_specs=(shard, shard, weight, weight, weight),
        check_vma=False,
    )
```

```python
import jax
import jax.numpy as jnp
from jax import lax
from jax.sharding import Mesh, PartitionSpec as P

EXPERTS = 4
TOK_GRP = 64
CAP = 48
F32 = jnp.float32
BF16 = jnp.bfloat16


def shift(n, k):
    return [(i, (i + k) % n) for i in range(n)]


def dot(a, b, dims):
    return lax.dot_general(a, b, (dims, ((), ())), preferred_element_type=F32)


def swap(a):
    return lax.ppermute(a, "core", [(0, 1), (1, 0)])


def body(tokens, d_out, scores, expert_ids, w_gate, w_up, w_down):
    nz, nx = lax.axis_size("z"), lax.axis_size("x")
    z, x, core = lax.axis_index("z"), lax.axis_index("x"), lax.axis_index("core")
    rows = tokens.shape[0]
    half = rows // 2
    hid = w_gate.shape[1]
    slots = CAP * 8
    block = nx * half
    mid = nz // 2

    def after(a, b):
        return lax.optimization_barrier((a, b))[0]

    gate_first = jax.nn.sigmoid(scores[:, 0] - scores[:, 1])
    gate_second = jax.nn.sigmoid(scores[:, 1] - scores[:, 0])
    labels = jnp.arange(EXPERTS, dtype=jnp.int32)
    chosen_first = (expert_ids[:, 0:1] == labels[None, :]).astype(jnp.int32)
    chosen_second = (expert_ids[:, 1:2] == labels[None, :]).astype(jnp.int32)
    counts = chosen_first + chosen_second
    earlier = jnp.arange(TOK_GRP)[:, None] > jnp.arange(TOK_GRP)[None, :]
    rank_table = dot(earlier.astype(BF16), counts.astype(BF16), ((1,), (0,))).astype(jnp.int32)
    slot_first = jnp.sum(rank_table * chosen_first, axis=1)
    slot_second = jnp.sum(rank_table * chosen_second, axis=1)
    place_first = expert_ids[:, 0] * CAP + slot_first
    place_second = expert_ids[:, 1] * CAP + slot_second
    places = jnp.arange(EXPERTS * CAP, dtype=jnp.int32)
    sel_first = place_first[:, None] == places[None, :]
    sel_second = place_second[:, None] == places[None, :]
    sel_both = (sel_first | sel_second).astype(BF16)
    slot_gate = jnp.sum(
        jnp.where(sel_first, gate_first[:, None], 0.0)
        + jnp.where(sel_second, gate_second[:, None], 0.0),
        axis=0,
    )
    scale = jnp.where(
        lax.broadcasted_iota(jnp.int32, (EXPERTS * CAP, 2 * half), 1) < half,
        1.0,
        slot_gate[:, None],
    )
    sent = []
    for part in range(2):
        own = slice(part * half, (part + 1) * half)
        both = jnp.concatenate([tokens[own], d_out[own]])
        sent.append((dot(sel_both, both, ((0,), (1,))) * scale).astype(BF16))
    sent = jnp.stack([a.reshape(EXPERTS, CAP, 2 * half) for a in sent], axis=1)
    sent = sent.reshape(EXPERTS * 2, CAP, 2 * half)
    got = lax.all_to_all(sent, ("y", "core"), 0, 0, tiled=True)
    w_gate, w_up, w_down = after((w_gate, w_up, w_down), got)
    eye = (
        lax.broadcasted_iota(jnp.int32, (slots, slots), 0)
        == lax.broadcasted_iota(jnp.int32, (slots, slots), 1)
    ).astype(BF16)
    shard = dot(got.reshape(slots, 2 * half), eye, ((0,), (0,))).astype(BF16)
    shard_t, shard_d = shard[:half], shard[half:]

    def prepare(w):
        parts = w.reshape(nz, nx, 2, half, hid)
        twice = jnp.concatenate([parts, parts], axis=1)

        def of(c):
            return lax.dynamic_slice(twice, (0, x, c, 0, 0), (nz, nx, 1, half, hid))[:, :, 0]

        return jnp.concatenate([of(core), swap(of(1 - core))], axis=-1)

    wg, wu = prepare(w_gate), prepare(w_up)
    near = 2
    wd = jnp.roll(prepare(w_down), near - z, axis=0)

    def at_z(a, j):
        return lax.dynamic_index_in_dim(a, lax.rem(z + j, nz), 0, keepdims=False)

    def of_z(w, j):
        return at_z(w, j).reshape(block, 2 * hid)

    def down(j):
        return wd[(j + near) % nz].reshape(block, 2 * hid)

    def right_of(a):
        return lax.ppermute(a, "z", shift(nz, 1))

    def left_of(a):
        return lax.ppermute(a, "z", shift(nz, -1))

    def finish(parts):
        mine = jnp.stack([p[:hid] for p in parts])
        return mine + swap(jnp.stack([p[hid:] for p in parts]))

    def share(own):
        return jnp.concatenate([own, swap(own)], axis=-2)

    pieces = [shard_t] + [lax.ppermute(shard_t, "x", shift(nx, -k)) for k in range(1, nx)]
    blocks = [None] * nz
    right = left = blocks[0] = jnp.concatenate(pieces + [shard_d])
    cut = (block + half) // 2
    reach = 2 * near + 1
    for k in range(1, mid):
        right, left = right_of(right), left_of(left)
        blocks[nz - k], blocks[k] = right, left
        if k == near:
            own_d = [jnp.concatenate([blocks[j - near][block:] for j in range(reach)])]
            far_d = [[lax.ppermute(own_d[0], "x", shift(nx, -k)) for k in range(1, nx)]]
    blocks[mid] = jnp.concatenate([right_of(right[:cut]), left_of(left[cut:])])

    own_d.append(jnp.concatenate([blocks[j - near][block:] for j in range(reach, nz)]))
    far_d.append([lax.ppermute(own_d[1], "x", shift(nx, -k)) for k in range(1, nx)])

    acts = [0.0, 0.0]
    full_t = jnp.zeros((nz, block, slots), BF16)
    order = [0] + [j for k in range(1, mid) for j in (nz - k, k)] + [mid]
    for j in order:
        t = blocks[j][:block]
        acts[0] = acts[0] + dot(of_z(wg, j), t, ((0,), (0,)))
        acts[1] = acts[1] + dot(of_z(wu, j), t, ((0,), (0,)))
        full_t = lax.dynamic_update_slice(full_t, t[None], (lax.rem(z + j, nz), 0, 0))
    full_t = full_t.reshape(-1, slots)
    act_gate, act_up = finish(acts)
    sig = jax.nn.sigmoid(act_gate)
    swished = act_gate * sig
    hidden = share((swished * act_up).astype(BF16))

    def reduce_z(made, hold):
        far_block = made(mid).astype(BF16)
        middle = far_block.shape[0] // 2
        right, left = right_of(far_block[:middle]), left_of(far_block[middle:])
        for k in range(mid - 1, 0, -1):
            to_right, to_left = made(k), made(nz - k)
            if k == mid - 1:
                to_right = jnp.concatenate(
                    [to_right[:middle] + right.astype(F32), to_right[middle:]]
                )
                to_left = jnp.concatenate(
                    [to_left[:middle], to_left[middle:] + left.astype(F32)]
                )
            else:
                to_right = to_right + right.astype(F32)
                to_left = to_left + left.astype(F32)
            to_right, to_left = to_right.astype(BF16), to_left.astype(BF16)
            hold(k, to_right, to_left)
            right, left = right_of(to_right), left_of(to_left)
        return made(0) + right.astype(F32) + left.astype(F32)

    def hold_d(k, right, left):
        if k == mid - 1:
            far_d[1] = after(far_d[1], (right, left))

    out_row = reduce_z(lambda j: dot(down(j), hidden, ((1,), (0,))), hold_d)
    all_d = [[own_d[i]] + list(far_d[i]) for i in range(2)]
    back_hidden = 0.0
    for i, some in ((0, slice(0, reach)), (1, slice(reach, nz))):
        for k in (0, 1, 3, 2):
            w = wd[some, k].reshape(-1, 2 * hid)
            back_hidden = back_hidden + dot(w, all_d[i][k], ((0,), (0,)))
    back_hidden = finish([back_hidden])[0]
    grad_act = (back_hidden * act_up * sig * (1.0 + act_gate * (1.0 - sig))).astype(BF16)
    grad_lin = (back_hidden * swished).astype(BF16)
    pair = share(jnp.stack([grad_act, grad_lin]))
    grad_act, grad_lin = pair[0], pair[1]

    def made_back(j):
        return dot(of_z(wg, j), grad_act, ((1,), (0,))) + dot(
            of_z(wu, j), grad_lin, ((1,), (0,))
        )

    for_grads = {}

    def hold_grads(k, right, left):
        if k == 2:
            for_grads[0] = after(grad_act, (right, left))
        if k == 1:
            for_grads[1], for_grads[2] = after((grad_lin, hidden), (right, left))

    back_row = reduce_z(made_back, hold_grads)

    rows_of = [
        jnp.concatenate([r[k * half : (k + 1) * half] for r in (out_row, back_row)])
        for k in range(nx)
    ]
    result = rows_of[0]
    for k in range(1, nx):
        piece = rows_of[k].astype(BF16)
        result = result + lax.ppermute(piece, "x", shift(nx, k)).astype(F32)
    result = result.astype(BF16)

    full_d = jnp.concatenate(
        [
            jnp.stack([d.reshape(-1, half, slots) for d in all_d[i]], axis=1)
            for i in range(2)
        ]
    ).reshape(-1, slots)
    which = lax.broadcasted_iota(jnp.int32, (nz, nx, 2, half, hid), 2)
    done = []
    for full, k in ((full_t, 0), (full_t, 1), (full_d, 2)):
        grad = dot(full, for_grads[k], ((1,), (1,))).astype(BF16)
        keep, give = grad[:, :hid], grad[:, hid:]
        keep, come = [
            jnp.roll(g.reshape(nz, nx, 1, half, hid), x, axis=1) for g in (keep, swap(give))
        ]
        if k == 2:
            keep, come = [jnp.roll(g, z - near, axis=0) for g in (keep, come)]
        done.append(jnp.where(which == core, keep, come).reshape(nz * nx * rows, hid))
    back_sent = dot(result, eye[: 2 * half, : 2 * half], ((0,), (0,))).astype(BF16)
    back_sent = back_sent.reshape(8, CAP, 2 * half)
    back_got = lax.all_to_all(back_sent, ("y", "core"), 0, 0, tiled=True)
    back_got = after(back_got, done).reshape(EXPERTS, 2, CAP, 2 * half)
    places_of = jnp.concatenate([sel_first.astype(BF16), sel_second.astype(BF16), sel_both])
    both = [
        dot(back_got[:, c].reshape(EXPERTS * CAP, 2 * half), places_of, ((0,), (1,)))
        for c in range(2)
    ]
    gates = jnp.concatenate([gate_first, gate_second])[None, :]
    weighed = [b[:half, : 2 * TOK_GRP] * gates for b in both]
    mixed = jnp.concatenate([w[:, :TOK_GRP] + w[:, TOK_GRP:] for w in weighed]).astype(BF16)
    d_tokens = jnp.concatenate([b[half:, 2 * TOK_GRP :] for b in both]).astype(BF16)
    return (mixed, d_tokens, done[0], done[1], done[2])


def solution(mesh):
    fine = Mesh(mesh.devices.reshape(4, 2, 8, 4), ("y", "core", "z", "x"))
    shard = P(("z", "x"), ("y", "core"))
    group = P(("y", "core"), None)
    weight = P(None, ("y", "core", "z", "x"))
    return jax.shard_map(
        body,
        mesh=fine,
        in_specs=(shard, shard, group, group, weight, weight, weight),
        out_specs=(shard, shard, weight, weight, weight),
        check_vma=False,
    )
```

```python
import jax
import jax.numpy as jnp
from jax import lax
from jax.sharding import Mesh, PartitionSpec as P

EXPERTS = 4
TOK_GRP = 64
CAP = 48
F32 = jnp.float32
BF16 = jnp.bfloat16


def shift(n, k):
    return [(i, (i + k) % n) for i in range(n)]


def dot(a, b, dims):
    return lax.dot_general(a, b, (dims, ((), ())), preferred_element_type=F32)


def swap(a):
    return lax.ppermute(a, "core", [(0, 1), (1, 0)])


def body(tokens, d_out, scores, expert_ids, w_gate, w_up, w_down):
    nz, nx = lax.axis_size("z"), lax.axis_size("x")
    z, x, core = lax.axis_index("z"), lax.axis_index("x"), lax.axis_index("core")
    rows = tokens.shape[0]
    half = rows // 2
    hid = w_gate.shape[1]
    slots = CAP * 8
    block = nx * half
    mid = nz // 2

    def after(a, b):
        return lax.optimization_barrier((a, b))[0]

    gate_first = jax.nn.sigmoid(scores[:, 0] - scores[:, 1])
    gate_second = jax.nn.sigmoid(scores[:, 1] - scores[:, 0])
    labels = jnp.arange(EXPERTS, dtype=jnp.int32)
    chosen_first = (expert_ids[:, 0:1] == labels[None, :]).astype(jnp.int32)
    chosen_second = (expert_ids[:, 1:2] == labels[None, :]).astype(jnp.int32)
    counts = chosen_first + chosen_second
    earlier = jnp.arange(TOK_GRP)[:, None] > jnp.arange(TOK_GRP)[None, :]
    rank_table = dot(earlier.astype(BF16), counts.astype(BF16), ((1,), (0,))).astype(jnp.int32)
    slot_first = jnp.sum(rank_table * chosen_first, axis=1)
    slot_second = jnp.sum(rank_table * chosen_second, axis=1)
    place_first = expert_ids[:, 0] * CAP + slot_first
    place_second = expert_ids[:, 1] * CAP + slot_second
    places = jnp.arange(EXPERTS * CAP, dtype=jnp.int32)
    sel_first = place_first[:, None] == places[None, :]
    sel_second = place_second[:, None] == places[None, :]
    sel_both = (sel_first | sel_second).astype(BF16)
    slot_gate = jnp.sum(
        jnp.where(sel_first, gate_first[:, None], 0.0)
        + jnp.where(sel_second, gate_second[:, None], 0.0),
        axis=0,
    )
    scale = jnp.where(
        lax.broadcasted_iota(jnp.int32, (EXPERTS * CAP, 2 * half), 1) < half,
        1.0,
        slot_gate[:, None],
    )
    sent = []
    for part in range(2):
        own = slice(part * half, (part + 1) * half)
        both = jnp.concatenate([tokens[own], d_out[own]])
        sent.append((dot(sel_both, both, ((0,), (1,))) * scale).astype(BF16))
    sent = jnp.stack([a.reshape(EXPERTS, CAP, 2 * half) for a in sent], axis=1)
    sent = sent.reshape(EXPERTS * 2, CAP, 2 * half)
    got = lax.all_to_all(sent, ("y", "core"), 0, 0, tiled=True)
    w_gate, w_up, w_down = after((w_gate, w_up, w_down), got)
    eye = (
        lax.broadcasted_iota(jnp.int32, (slots, slots), 0)
        == lax.broadcasted_iota(jnp.int32, (slots, slots), 1)
    ).astype(BF16)
    shard = dot(got.reshape(slots, 2 * half), eye, ((0,), (0,))).astype(BF16)
    shard_t, shard_d = shard[:half], shard[half:]

    def prepare(w):
        parts = w.reshape(nz, nx, 2, half, hid)
        twice = jnp.concatenate([parts, parts], axis=1)

        def of(c):
            return lax.dynamic_slice(twice, (0, x, c, 0, 0), (nz, nx, 1, half, hid))[:, :, 0]

        return jnp.concatenate([of(core), swap(of(1 - core))], axis=-1)

    wg, wu = prepare(w_gate), prepare(w_up)
    near = 2
    wd = jnp.roll(prepare(w_down), near - z, axis=0)

    def at_z(a, j):
        return lax.dynamic_index_in_dim(a, lax.rem(z + j, nz), 0, keepdims=False)

    def of_z(w, j):
        return at_z(w, j).reshape(block, 2 * hid)

    def down(j):
        return wd[(j + near) % nz].reshape(block, 2 * hid)

    def right_of(a):
        return lax.ppermute(a, "z", shift(nz, 1))

    def left_of(a):
        return lax.ppermute(a, "z", shift(nz, -1))

    def finish(parts):
        mine = jnp.stack([p[:hid] for p in parts])
        return mine + swap(jnp.stack([p[hid:] for p in parts]))

    def share(own):
        return jnp.concatenate([own, swap(own)], axis=-2)

    pieces = [shard_t] + [lax.ppermute(shard_t, "x", shift(nx, -k)) for k in range(1, nx)]
    blocks = [None] * nz
    right = left = blocks[0] = jnp.concatenate(pieces + [shard_d])
    cut = (block + half) // 2
    reach = 2 * near + 1
    for k in range(1, mid):
        right, left = right_of(right), left_of(left)
        blocks[nz - k], blocks[k] = right, left
        if k == near:
            own_d = [jnp.concatenate([blocks[j - near][block:] for j in range(reach)])]
            far_d = [[lax.ppermute(own_d[0], "x", shift(nx, -k)) for k in range(1, nx)]]
    blocks[mid] = jnp.concatenate([right_of(right[:cut]), left_of(left[cut:])])

    own_d.append(jnp.concatenate([blocks[j - near][block:] for j in range(reach, nz)]))
    far_d.append([lax.ppermute(own_d[1], "x", shift(nx, -k)) for k in range(1, nx)])

    acts = [0.0, 0.0]
    full_t = jnp.zeros((nz, block, slots), BF16)
    order = [0] + [j for k in range(1, mid) for j in (nz - k, k)] + [mid]
    for j in order:
        t = blocks[j][:block]
        acts[0] = acts[0] + dot(of_z(wg, j), t, ((0,), (0,)))
        acts[1] = acts[1] + dot(of_z(wu, j), t, ((0,), (0,)))
        full_t = lax.dynamic_update_slice(full_t, t[None], (lax.rem(z + j, nz), 0, 0))
    full_t = full_t.reshape(-1, slots)
    act_gate, act_up = finish(acts)
    sig = jax.nn.sigmoid(act_gate)
    swished = act_gate * sig
    hidden = share((swished * act_up).astype(BF16))

    def reduce_z(made, hold):
        far_block = made(mid).astype(BF16)
        middle = far_block.shape[0] // 2
        right, left = right_of(far_block[:middle]), left_of(far_block[middle:])
        for k in range(mid - 1, 0, -1):
            to_right, to_left = made(k), made(nz - k)
            if k == mid - 1:
                to_right = jnp.concatenate(
                    [to_right[:middle] + right.astype(F32), to_right[middle:]]
                )
                to_left = jnp.concatenate(
                    [to_left[:middle], to_left[middle:] + left.astype(F32)]
                )
            else:
                to_right = to_right + right.astype(F32)
                to_left = to_left + left.astype(F32)
            to_right, to_left = to_right.astype(BF16), to_left.astype(BF16)
            hold(k, to_right, to_left)
            right, left = right_of(to_right), left_of(to_left)
        return made(0) + right.astype(F32) + left.astype(F32)

    def hold_d(k, right, left):
        if k == mid - 1:
            far_d[1] = after(far_d[1], (right, left))

    out_row = reduce_z(lambda j: dot(down(j), hidden, ((1,), (0,))), hold_d)
    all_d = [[own_d[i]] + list(far_d[i]) for i in range(2)]
    back_hidden = 0.0
    for i, some in ((0, slice(0, reach)), (1, slice(reach, nz))):
        for k in (0, 1, 3, 2):
            w = wd[some, k].reshape(-1, 2 * hid)
            back_hidden = back_hidden + dot(w, all_d[i][k], ((0,), (0,)))
    back_hidden = finish([back_hidden])[0]
    grad_act = (back_hidden * act_up * sig * (1.0 + act_gate * (1.0 - sig))).astype(BF16)
    grad_lin = (back_hidden * swished).astype(BF16)
    pair = share(jnp.stack([grad_act, grad_lin]))
    grad_act, grad_lin = pair[0], pair[1]

    def made_back(j):
        return dot(of_z(wg, j), grad_act, ((1,), (0,))) + dot(
            of_z(wu, j), grad_lin, ((1,), (0,))
        )

    for_grads = {}

    def hold_grads(k, right, left):
        if k == 2:
            for_grads["down"] = after(hidden, (right, left))
        if k == 1:
            for_grads["act"] = after((grad_act, grad_lin), (right, left))

    back_row = reduce_z(made_back, hold_grads)

    rows_of = [
        jnp.concatenate([r[k * half : (k + 1) * half] for r in (out_row, back_row)])
        for k in range(nx)
    ]
    result = rows_of[0]
    sends = lax.optimization_barrier([r.astype(BF16) for r in rows_of[1:]])
    for k in range(1, nx):
        result = result + lax.ppermute(sends[k - 1], "x", shift(nx, k)).astype(F32)
    result = result.astype(BF16)

    full_d = jnp.concatenate(
        [
            jnp.stack([d.reshape(-1, half, slots) for d in all_d[i]], axis=1)
            for i in range(2)
        ]
    ).reshape(-1, slots)
    which = lax.broadcasted_iota(jnp.int32, (nz, nx, 2, half, hid), 2)
    grad_act, grad_lin = for_grads["act"]
    both = jnp.concatenate([grad_act[:hid], grad_lin[:hid], grad_act[hid:], grad_lin[hid:]])
    parts = []
    for full, g in ((full_d, for_grads["down"]), (full_t, both)):
        grad = dot(full, g, ((1,), (1,))).astype(BF16)
        width = g.shape[0] // 2
        keep, come = grad[:, :width], swap(grad[:, width:])
        for i in range(0, width, hid):
            parts.append(
                [
                    jnp.roll(p[:, i : i + hid].reshape(nz, nx, 1, half, hid), x, axis=1)
                    for p in (keep, come)
                ]
            )
    parts[0] = [jnp.roll(p, z - near, axis=0) for p in parts[0]]
    done = [
        jnp.where(which == core, keep, come).reshape(nz * nx * rows, hid)
        for keep, come in parts[1:] + parts[:1]
    ]

    back_sent = dot(result, eye[: 2 * half, : 2 * half], ((0,), (0,))).astype(BF16)
    back_sent = back_sent.reshape(8, CAP, 2 * half)
    back_got = lax.all_to_all(back_sent, ("y", "core"), 0, 0, tiled=True)
    back_got = after(back_got, done).reshape(EXPERTS, 2, CAP, 2 * half)
    places_of = jnp.concatenate([sel_first.astype(BF16), sel_second.astype(BF16), sel_both])
    both = [
        dot(places_of, back_got[:, c].reshape(EXPERTS * CAP, 2 * half), ((1,), (0,)))
        for c in range(2)
    ]
    out = jnp.concatenate([b[: 2 * TOK_GRP, :half] for b in both], axis=1)
    mixed = out[:TOK_GRP] * gate_first[:, None] + out[TOK_GRP:] * gate_second[:, None]
    mixed = mixed.astype(BF16).T
    d_tokens = jnp.concatenate([b[2 * TOK_GRP :, half:] for b in both], axis=1)
    d_tokens = d_tokens.astype(BF16).T
    return (mixed, d_tokens, done[0], done[1], done[2])


def solution(mesh):
    fine = Mesh(mesh.devices.reshape(4, 2, 8, 4), ("y", "core", "z", "x"))
    shard = P(("z", "x"), ("y", "core"))
    group = P(("y", "core"), None)
    weight = P(None, ("y", "core", "z", "x"))
    return jax.shard_map(
        body,
        mesh=fine,
        in_specs=(shard, shard, group, group, weight, weight, weight),
        out_specs=(shard, shard, weight, weight, weight),
        check_vma=False,
    )
```

```python
import jax
import jax.numpy as jnp
from jax import lax
from jax.experimental import pallas as pl
from jax.sharding import Mesh, PartitionSpec as P

EXPERTS = 4
TOK_GRP = 64
CAP = 48
F32 = jnp.float32
BF16 = jnp.bfloat16


def shift(n, k):
    return [(i, (i + k) % n) for i in range(n)]


def dot(a, b, dims):
    return lax.dot_general(a, b, (dims, ((), ())), preferred_element_type=F32)


def swap(a):
    return lax.ppermute(a, "core", [(0, 1), (1, 0)])


def dispatch_kernel(tok_ref, cot_ref, score_ref, id_ref, sent_ref, first_ref, second_ref, gate_ref):
    places, rows = first_ref.shape[0], tok_ref.shape[1]
    half = rows // 2
    iota = lax.broadcasted_iota
    id_first, id_second = id_ref[0:1, :], id_ref[1:2, :]
    gate_first = jax.nn.sigmoid(score_ref[0:1, :] - score_ref[1:2, :])
    gate_second = jax.nn.sigmoid(score_ref[1:2, :] - score_ref[0:1, :])
    gate_ref[0:1, :] = gate_first
    gate_ref[1:2, :] = gate_second
    labels = iota(jnp.int32, (8, TOK_GRP), 0)
    is_first, is_second = labels == id_first, labels == id_second
    counts = (is_first | is_second).astype(F32).astype(BF16)
    square = (TOK_GRP, TOK_GRP)
    earlier = (iota(jnp.int32, square, 0) < iota(jnp.int32, square, 1)).astype(F32).astype(BF16)
    rank = dot(counts, earlier, ((1,), (0,)))
    rank_first = jnp.sum(jnp.where(is_first, rank, 0.0), axis=0, keepdims=True)
    rank_second = jnp.sum(jnp.where(is_second, rank, 0.0), axis=0, keepdims=True)
    place = iota(jnp.int32, (places, TOK_GRP), 0)
    first = place == id_first * CAP + rank_first.astype(jnp.int32)
    second = place == id_second * CAP + rank_second.astype(jnp.int32)
    first_f, second_f = first.astype(F32), second.astype(F32)
    first_ref[...] = first_f.astype(BF16)
    second_ref[...] = second_f.astype(BF16)
    both = (first_f + second_f).astype(BF16)
    scale = jnp.where(first, gate_first, 0.0) + jnp.where(second, gate_second, 0.0)
    scale = jnp.sum(scale, axis=1, keepdims=True)
    tok = dot(both, tok_ref[...], ((1,), (0,))).astype(BF16)
    cot = (dot(both, cot_ref[...], ((1,), (0,))) * scale).astype(BF16)
    src, dst = iota(jnp.int32, (rows, rows), 0), iota(jnp.int32, (rows, rows), 1)
    for c in range(2):
        front = ((src - c * half == dst) & (dst < half)).astype(F32).astype(BF16)
        behind = ((src - c * half == dst - half) & (dst >= half)).astype(F32).astype(BF16)
        moved = dot(tok, front, ((1,), (0,))) + dot(cot, behind, ((1,), (0,)))
        moved = moved.astype(BF16)
        for e in range(EXPERTS):
            sent_ref[2 * e + c] = moved[e * CAP : (e + 1) * CAP]


def dispatch(tok, cot, scores, ids):
    places = EXPERTS * CAP
    return pl.pallas_call(
        dispatch_kernel,
        out_shape=(
            jax.ShapeDtypeStruct((EXPERTS * 2, CAP, tok.shape[1]), BF16),
            jax.ShapeDtypeStruct((places, TOK_GRP), BF16),
            jax.ShapeDtypeStruct((places, TOK_GRP), BF16),
            jax.ShapeDtypeStruct((2, TOK_GRP), F32),
        ),
    )(tok, cot, scores, ids)


def body(tokens, d_out, scores, expert_ids, w_gate, w_up, w_down):
    nz, nx = lax.axis_size("z"), lax.axis_size("x")
    z, x, core = lax.axis_index("z"), lax.axis_index("x"), lax.axis_index("core")
    rows = tokens.shape[0]
    half = rows // 2
    hid = w_gate.shape[1]
    slots = CAP * 8
    block = nx * half
    mid = nz // 2

    def after(a, b):
        return lax.optimization_barrier((a, b))[0]

    sent, sel_first, sel_second, gates = dispatch(tokens.T, d_out.T, scores.T, expert_ids.T)
    got = lax.all_to_all(sent, ("y", "core"), 0, 0, tiled=True)
    w_gate, w_up, w_down = after((w_gate, w_up, w_down), got)
    eye = (
        lax.broadcasted_iota(jnp.int32, (slots, slots), 0)
        == lax.broadcasted_iota(jnp.int32, (slots, slots), 1)
    ).astype(BF16)
    shard = dot(got.reshape(slots, 2 * half), eye, ((0,), (0,))).astype(BF16)
    shard_t, shard_d = shard[:half], shard[half:]

    def prepare(w):
        parts = w.reshape(nz, nx, 2, half, hid)
        twice = jnp.concatenate([parts, parts], axis=1)

        def of(c):
            return lax.dynamic_slice(twice, (0, x, c, 0, 0), (nz, nx, 1, half, hid))[:, :, 0]

        return jnp.concatenate([of(core), swap(of(1 - core))], axis=-1)

    wg, wu = prepare(w_gate), prepare(w_up)
    near = 2
    wd = jnp.roll(prepare(w_down), near - z, axis=0)

    def at_z(a, j):
        return lax.dynamic_index_in_dim(a, lax.rem(z + j, nz), 0, keepdims=False)

    def of_z(w, j):
        return at_z(w, j).reshape(block, 2 * hid)

    def down(j):
        return wd[(j + near) % nz].reshape(block, 2 * hid)

    def right_of(a):
        return lax.ppermute(a, "z", shift(nz, 1))

    def left_of(a):
        return lax.ppermute(a, "z", shift(nz, -1))

    def finish(parts):
        mine = jnp.stack([p[:hid] for p in parts])
        return mine + swap(jnp.stack([p[hid:] for p in parts]))

    def share(own):
        return jnp.concatenate([own, swap(own)], axis=-2)

    pieces = [shard_t] + [lax.ppermute(shard_t, "x", shift(nx, -k)) for k in range(1, nx)]
    blocks = [None] * nz
    right = left = blocks[0] = jnp.concatenate(pieces + [shard_d])
    cut = (block + half) // 2
    reach = 2 * near + 1
    for k in range(1, mid):
        right, left = right_of(right), left_of(left)
        blocks[nz - k], blocks[k] = right, left
        if k == near:
            own_d = [jnp.concatenate([blocks[j - near][block:] for j in range(reach)])]
            far_d = [[lax.ppermute(own_d[0], "x", shift(nx, -k)) for k in range(1, nx)]]
    blocks[mid] = jnp.concatenate([right_of(right[:cut]), left_of(left[cut:])])

    own_d.append(jnp.concatenate([blocks[j - near][block:] for j in range(reach, nz)]))
    far_d.append([lax.ppermute(own_d[1], "x", shift(nx, -k)) for k in range(1, nx)])

    acts = [0.0, 0.0]
    full_t = jnp.zeros((nz, block, slots), BF16)
    order = [0] + [j for k in range(1, mid) for j in (nz - k, k)] + [mid]
    for j in order:
        t = blocks[j][:block]
        acts[0] = acts[0] + dot(of_z(wg, j), t, ((0,), (0,)))
        acts[1] = acts[1] + dot(of_z(wu, j), t, ((0,), (0,)))
        full_t = lax.dynamic_update_slice(full_t, t[None], (lax.rem(z + j, nz), 0, 0))
    full_t = full_t.reshape(-1, slots)
    act_gate, act_up = finish(acts)
    sig = jax.nn.sigmoid(act_gate)
    swished = act_gate * sig
    hidden = share((swished * act_up).astype(BF16))

    def reduce_z(made, hold):
        far_block = made(mid).astype(BF16)
        middle = far_block.shape[0] // 2
        right, left = right_of(far_block[:middle]), left_of(far_block[middle:])
        for k in range(mid - 1, 0, -1):
            to_right, to_left = made(k), made(nz - k)
            if k == mid - 1:
                to_right = jnp.concatenate(
                    [to_right[:middle] + right.astype(F32), to_right[middle:]]
                )
                to_left = jnp.concatenate(
                    [to_left[:middle], to_left[middle:] + left.astype(F32)]
                )
            else:
                to_right = to_right + right.astype(F32)
                to_left = to_left + left.astype(F32)
            to_right, to_left = to_right.astype(BF16), to_left.astype(BF16)
            hold(k, to_right, to_left)
            right, left = right_of(to_right), left_of(to_left)
        return made(0) + right.astype(F32) + left.astype(F32)

    def hold_d(k, right, left):
        if k == mid - 1:
            far_d[1] = after(far_d[1], (right, left))

    out_row = reduce_z(lambda j: dot(down(j), hidden, ((1,), (0,))), hold_d)
    all_d = [[own_d[i]] + list(far_d[i]) for i in range(2)]
    back_hidden = 0.0
    for i, some in ((0, slice(0, reach)), (1, slice(reach, nz))):
        for k in (0, 1, 3, 2):
            w = wd[some, k].reshape(-1, 2 * hid)
            back_hidden = back_hidden + dot(w, all_d[i][k], ((0,), (0,)))
    back_hidden = finish([back_hidden])[0]
    grad_act = (back_hidden * act_up * sig * (1.0 + act_gate * (1.0 - sig))).astype(BF16)
    grad_lin = (back_hidden * swished).astype(BF16)
    pair = share(jnp.stack([grad_act, grad_lin]))
    grad_act, grad_lin = pair[0], pair[1]

    def made_back(j):
        return dot(of_z(wg, j), grad_act, ((1,), (0,))) + dot(
            of_z(wu, j), grad_lin, ((1,), (0,))
        )

    for_grads = {}

    def hold_grads(k, right, left):
        if k == 2:
            for_grads["down"] = after(hidden, (right, left))
        if k == 1:
            for_grads["act"] = after((grad_act, grad_lin), (right, left))

    back_row = reduce_z(made_back, hold_grads)

    rows_of = [
        jnp.concatenate([r[k * half : (k + 1) * half] for r in (out_row, back_row)])
        for k in range(nx)
    ]
    result = rows_of[0]
    sends = lax.optimization_barrier([r.astype(BF16) for r in rows_of[1:]])
    for k in range(1, nx):
        result = result + lax.ppermute(sends[k - 1], "x", shift(nx, k)).astype(F32)
    result = result.astype(BF16)

    full_d = jnp.concatenate(
        [
            jnp.stack([d.reshape(-1, half, slots) for d in all_d[i]], axis=1)
            for i in range(2)
        ]
    ).reshape(-1, slots)
    which = lax.broadcasted_iota(jnp.int32, (nz, nx, 2, half, hid), 2)
    grad_act, grad_lin = for_grads["act"]
    both = jnp.concatenate([grad_act[:hid], grad_lin[:hid], grad_act[hid:], grad_lin[hid:]])
    parts = []
    for full, g in ((full_d, for_grads["down"]), (full_t, both)):
        grad = dot(full, g, ((1,), (1,))).astype(BF16)
        width = g.shape[0] // 2
        keep, come = grad[:, :width], swap(grad[:, width:])
        for i in range(0, width, hid):
            parts.append(
                [
                    jnp.roll(p[:, i : i + hid].reshape(nz, nx, 1, half, hid), x, axis=1)
                    for p in (keep, come)
                ]
            )
    parts[0] = [jnp.roll(p, z - near, axis=0) for p in parts[0]]
    done = [
        jnp.where(which == core, keep, come).reshape(nz * nx * rows, hid)
        for keep, come in parts[1:] + parts[:1]
    ]

    back_sent = dot(result, eye[: 2 * half, : 2 * half], ((0,), (0,))).astype(BF16)
    back_sent = back_sent.reshape(8, CAP, 2 * half)
    back_got = lax.all_to_all(back_sent, ("y", "core"), 0, 0, tiled=True)
    back_got = after(back_got, done).reshape(EXPERTS, 2, CAP, 2 * half)
    places_of = jnp.concatenate([sel_first, sel_second, sel_first + sel_second], axis=1)
    both = [
        dot(places_of, back_got[:, c].reshape(EXPERTS * CAP, 2 * half), ((0,), (0,)))
        for c in range(2)
    ]
    out = jnp.concatenate([b[: 2 * TOK_GRP, :half] for b in both], axis=1)
    mixed = out[:TOK_GRP] * gates[0][:, None] + out[TOK_GRP:] * gates[1][:, None]
    mixed = mixed.astype(BF16).T
    d_tokens = jnp.concatenate([b[2 * TOK_GRP :, half:] for b in both], axis=1)
    d_tokens = d_tokens.astype(BF16).T
    return (mixed, d_tokens, done[0], done[1], done[2])


def solution(mesh):
    fine = Mesh(mesh.devices.reshape(4, 2, 8, 4), ("y", "core", "z", "x"))
    shard = P(("z", "x"), ("y", "core"))
    group = P(("y", "core"), None)
    weight = P(None, ("y", "core", "z", "x"))
    return jax.shard_map(
        body,
        mesh=fine,
        in_specs=(shard, shard, group, group, weight, weight, weight),
        out_specs=(shard, shard, weight, weight, weight),
        check_vma=False,
    )
```

```python
import jax
import jax.numpy as jnp
from jax import lax
from jax.experimental import pallas as pl
from jax.sharding import Mesh, PartitionSpec as P

EXPERTS = 4
TOK_GRP = 64
CAP = 48
F32 = jnp.float32
BF16 = jnp.bfloat16


def shift(n, k):
    return [(i, (i + k) % n) for i in range(n)]


def dot(a, b, dims):
    return lax.dot_general(a, b, (dims, ((), ())), preferred_element_type=F32)


def swap(a):
    return lax.ppermute(a, "core", [(0, 1), (1, 0)])


def dispatch_kernel(tok_ref, cot_ref, score_ref, id_ref, sent_ref, first_ref, second_ref, gate_ref):
    places, rows = first_ref.shape[0], tok_ref.shape[1]
    half = rows // 2
    iota = lax.broadcasted_iota
    id_first, id_second = id_ref[0:1, :], id_ref[1:2, :]
    gate_first = jax.nn.sigmoid(score_ref[0:1, :] - score_ref[1:2, :])
    gate_second = jax.nn.sigmoid(score_ref[1:2, :] - score_ref[0:1, :])
    gate_ref[0:1, :] = gate_first
    gate_ref[1:2, :] = gate_second
    labels = iota(jnp.int32, (8, TOK_GRP), 0)
    is_first, is_second = labels == id_first, labels == id_second
    counts = (is_first | is_second).astype(F32).astype(BF16)
    square = (TOK_GRP, TOK_GRP)
    earlier = (iota(jnp.int32, square, 0) < iota(jnp.int32, square, 1)).astype(F32).astype(BF16)
    rank = dot(counts, earlier, ((1,), (0,)))
    rank_first = jnp.sum(jnp.where(is_first, rank, 0.0), axis=0, keepdims=True)
    rank_second = jnp.sum(jnp.where(is_second, rank, 0.0), axis=0, keepdims=True)
    place = iota(jnp.int32, (places, TOK_GRP), 0)
    first = place == id_first * CAP + rank_first.astype(jnp.int32)
    second = place == id_second * CAP + rank_second.astype(jnp.int32)
    first_f, second_f = first.astype(F32), second.astype(F32)
    first_ref[...] = first_f.astype(BF16)
    second_ref[...] = second_f.astype(BF16)
    both = (first_f + second_f).astype(BF16)
    scale = jnp.where(first, gate_first, 0.0) + jnp.where(second, gate_second, 0.0)
    scale = jnp.sum(scale, axis=1, keepdims=True)
    tok = dot(both, tok_ref[...], ((1,), (0,))).astype(BF16)
    cot = (dot(both, cot_ref[...], ((1,), (0,))) * scale).astype(BF16)
    src, dst = iota(jnp.int32, (rows, rows), 0), iota(jnp.int32, (rows, rows), 1)
    for c in range(2):
        front = ((src - c * half == dst) & (dst < half)).astype(F32).astype(BF16)
        behind = ((src - c * half == dst - half) & (dst >= half)).astype(F32).astype(BF16)
        moved = dot(tok, front, ((1,), (0,))) + dot(cot, behind, ((1,), (0,)))
        moved = moved.astype(BF16)
        for e in range(EXPERTS):
            sent_ref[2 * e + c] = moved[e * CAP : (e + 1) * CAP]


def dispatch(tok, cot, scores, ids):
    places = EXPERTS * CAP
    return pl.pallas_call(
        dispatch_kernel,
        out_shape=(
            jax.ShapeDtypeStruct((EXPERTS * 2, CAP, tok.shape[1]), BF16),
            jax.ShapeDtypeStruct((places, TOK_GRP), BF16),
            jax.ShapeDtypeStruct((places, TOK_GRP), BF16),
            jax.ShapeDtypeStruct((2, TOK_GRP), F32),
        ),
    )(tok, cot, scores, ids)


def fold_kernel(own_ref, *refs):
    total = own_ref[...]
    for ref in refs[:-1]:
        total = total + ref[...].astype(F32)
    square = (total.shape[0],) * 2
    same = lax.broadcasted_iota(jnp.int32, square, 0) == lax.broadcasted_iota(jnp.int32, square, 1)
    turned = dot(total.astype(BF16), same.astype(F32).astype(BF16), ((0,), (0,))).astype(BF16)
    for g in range(8):
        refs[-1][g] = turned[g * CAP : (g + 1) * CAP]


def fold(own, come):
    shape = jax.ShapeDtypeStruct((8, CAP, own.shape[0]), BF16)
    return pl.pallas_call(fold_kernel, out_shape=shape)(own, *come)


def body(tokens, d_out, scores, expert_ids, w_gate, w_up, w_down):
    nz, nx = lax.axis_size("z"), lax.axis_size("x")
    z, x, core = lax.axis_index("z"), lax.axis_index("x"), lax.axis_index("core")
    rows = tokens.shape[0]
    half = rows // 2
    hid = w_gate.shape[1]
    slots = CAP * 8
    block = nx * half
    mid = nz // 2

    def after(a, b):
        return lax.optimization_barrier((a, b))[0]

    sent, sel_first, sel_second, gates = dispatch(tokens.T, d_out.T, scores.T, expert_ids.T)
    got = lax.all_to_all(sent, ("y", "core"), 0, 0, tiled=True)
    w_gate, w_up, w_down = after((w_gate, w_up, w_down), got)
    eye = (
        lax.broadcasted_iota(jnp.int32, (slots, slots), 0)
        == lax.broadcasted_iota(jnp.int32, (slots, slots), 1)
    ).astype(BF16)
    shard = dot(got.reshape(slots, 2 * half), eye, ((0,), (0,))).astype(BF16)
    shard_t, shard_d = shard[:half], shard[half:]

    def prepare(w):
        parts = w.reshape(nz, nx, 2, half, hid)
        twice = jnp.concatenate([parts, parts], axis=1)

        def of(c):
            return lax.dynamic_slice(twice, (0, x, c, 0, 0), (nz, nx, 1, half, hid))[:, :, 0]

        return jnp.concatenate([of(core), swap(of(1 - core))], axis=-1)

    wg, wu = prepare(w_gate), prepare(w_up)
    near = 2
    wd = jnp.roll(prepare(w_down), near - z, axis=0)

    def at_z(a, j):
        return lax.dynamic_index_in_dim(a, lax.rem(z + j, nz), 0, keepdims=False)

    def of_z(w, j):
        return at_z(w, j).reshape(block, 2 * hid)

    def down(j):
        return wd[(j + near) % nz].reshape(block, 2 * hid)

    def right_of(a):
        return lax.ppermute(a, "z", shift(nz, 1))

    def left_of(a):
        return lax.ppermute(a, "z", shift(nz, -1))

    def finish(parts):
        mine = jnp.stack([p[:hid] for p in parts])
        return mine + swap(jnp.stack([p[hid:] for p in parts]))

    def share(own):
        return jnp.concatenate([own, swap(own)], axis=-2)

    pieces = [shard_t] + [lax.ppermute(shard_t, "x", shift(nx, -k)) for k in range(1, nx)]
    blocks = [None] * nz
    right = left = blocks[0] = jnp.concatenate(pieces + [shard_d])
    cut = (block + half) // 2
    reach = 2 * near + 1
    for k in range(1, mid):
        right, left = right_of(right), left_of(left)
        blocks[nz - k], blocks[k] = right, left
        if k == near:
            own_d = [jnp.concatenate([blocks[j - near][block:] for j in range(reach)])]
            far_d = [[lax.ppermute(own_d[0], "x", shift(nx, -k)) for k in range(1, nx)]]
    blocks[mid] = jnp.concatenate([right_of(right[:cut]), left_of(left[cut:])])

    own_d.append(jnp.concatenate([blocks[j - near][block:] for j in range(reach, nz)]))
    far_d.append([lax.ppermute(own_d[1], "x", shift(nx, -k)) for k in range(1, nx)])

    acts = [0.0, 0.0]
    full_t = jnp.zeros((nz, block, slots), BF16)
    order = [0] + [j for k in range(1, mid) for j in (nz - k, k)] + [mid]
    for j in order:
        t = blocks[j][:block]
        acts[0] = acts[0] + dot(of_z(wg, j), t, ((0,), (0,)))
        acts[1] = acts[1] + dot(of_z(wu, j), t, ((0,), (0,)))
        full_t = lax.dynamic_update_slice(full_t, t[None], (lax.rem(z + j, nz), 0, 0))
    full_t = full_t.reshape(-1, slots)
    act_gate, act_up = finish(acts)
    sig = jax.nn.sigmoid(act_gate)
    swished = act_gate * sig
    hidden = share((swished * act_up).astype(BF16))

    def reduce_z(made, hold):
        far_block = made(mid).astype(BF16)
        middle = far_block.shape[0] // 2
        right, left = right_of(far_block[:middle]), left_of(far_block[middle:])
        for k in range(mid - 1, 0, -1):
            to_right, to_left = made(k), made(nz - k)
            if k == mid - 1:
                to_right = jnp.concatenate(
                    [to_right[:middle] + right.astype(F32), to_right[middle:]]
                )
                to_left = jnp.concatenate(
                    [to_left[:middle], to_left[middle:] + left.astype(F32)]
                )
            else:
                to_right = to_right + right.astype(F32)
                to_left = to_left + left.astype(F32)
            to_right, to_left = to_right.astype(BF16), to_left.astype(BF16)
            hold(k, to_right, to_left)
            right, left = right_of(to_right), left_of(to_left)
        return made(0) + right.astype(F32) + left.astype(F32)

    def hold_d(k, right, left):
        if k == mid - 1:
            far_d[1] = after(far_d[1], (right, left))

    out_row = reduce_z(lambda j: dot(down(j), hidden, ((1,), (0,))), hold_d)
    all_d = [[own_d[i]] + list(far_d[i]) for i in range(2)]
    back_hidden = 0.0
    for i, some in ((0, slice(0, reach)), (1, slice(reach, nz))):
        for k in (0, 1, 3, 2):
            w = wd[some, k].reshape(-1, 2 * hid)
            back_hidden = back_hidden + dot(w, all_d[i][k], ((0,), (0,)))
    back_hidden = finish([back_hidden])[0]
    grad_act = (back_hidden * act_up * sig * (1.0 + act_gate * (1.0 - sig))).astype(BF16)
    grad_lin = (back_hidden * swished).astype(BF16)
    pair = share(jnp.stack([grad_act, grad_lin]))
    grad_act, grad_lin = pair[0], pair[1]

    def made_back(j):
        return dot(of_z(wg, j), grad_act, ((1,), (0,))) + dot(
            of_z(wu, j), grad_lin, ((1,), (0,))
        )

    for_grads = {}

    def hold_grads(k, right, left):
        if k == 2:
            for_grads["down"] = after(hidden, (right, left))
        if k == 1:
            for_grads["act"] = after((grad_act, grad_lin), (right, left))

    back_row = reduce_z(made_back, hold_grads)

    rows_of = [
        jnp.concatenate([r[k * half : (k + 1) * half] for r in (out_row, back_row)])
        for k in range(nx)
    ]
    result = rows_of[0]
    sends = lax.optimization_barrier([r.astype(BF16) for r in rows_of[1:]])
    arrived = [lax.ppermute(sends[k - 1], "x", shift(nx, k)) for k in range(1, nx)]

    full_d = jnp.concatenate(
        [
            jnp.stack([d.reshape(-1, half, slots) for d in all_d[i]], axis=1)
            for i in range(2)
        ]
    ).reshape(-1, slots)
    which = lax.broadcasted_iota(jnp.int32, (nz, nx, 2, half, hid), 2)
    grad_act, grad_lin = for_grads["act"]
    both = jnp.concatenate([grad_act[:hid], grad_lin[:hid], grad_act[hid:], grad_lin[hid:]])
    parts = []
    for full, g in ((full_d, for_grads["down"]), (full_t, both)):
        grad = dot(full, g, ((1,), (1,))).astype(BF16)
        width = g.shape[0] // 2
        keep, come = grad[:, :width], swap(grad[:, width:])
        for i in range(0, width, hid):
            parts.append(
                [
                    jnp.roll(p[:, i : i + hid].reshape(nz, nx, 1, half, hid), x, axis=1)
                    for p in (keep, come)
                ]
            )
    parts[0] = [jnp.roll(p, z - near, axis=0) for p in parts[0]]
    done = [
        jnp.where(which == core, keep, come).reshape(nz * nx * rows, hid)
        for keep, come in parts[1:] + parts[:1]
    ]

    back_sent = fold(result, arrived)
    back_got = lax.all_to_all(back_sent, ("y", "core"), 0, 0, tiled=True)
    back_got = after(back_got, done).reshape(EXPERTS, 2, CAP, 2 * half)
    places_of = jnp.concatenate([sel_first, sel_second, sel_first + sel_second], axis=1)
    both = [
        dot(places_of, back_got[:, c].reshape(EXPERTS * CAP, 2 * half), ((0,), (0,)))
        for c in range(2)
    ]
    out = jnp.concatenate([b[: 2 * TOK_GRP, :half] for b in both], axis=1)
    mixed = out[:TOK_GRP] * gates[0][:, None] + out[TOK_GRP:] * gates[1][:, None]
    mixed = mixed.astype(BF16).T
    d_tokens = jnp.concatenate([b[2 * TOK_GRP :, half:] for b in both], axis=1)
    d_tokens = d_tokens.astype(BF16).T
    return (mixed, d_tokens, done[0], done[1], done[2])


def solution(mesh):
    fine = Mesh(mesh.devices.reshape(4, 2, 8, 4), ("y", "core", "z", "x"))
    shard = P(("z", "x"), ("y", "core"))
    group = P(("y", "core"), None)
    weight = P(None, ("y", "core", "z", "x"))
    return jax.shard_map(
        body,
        mesh=fine,
        in_specs=(shard, shard, group, group, weight, weight, weight),
        out_specs=(shard, shard, weight, weight, weight),
        check_vma=False,
    )
```
